256 devices in a mesh: ctx: 4 (over y), tp: 8 (over z), ep: 8 (over x, core).
Axes of the slice: x: 4, y: 4, z: 8, core: 2. Of those that a mesh axis runs over, the one named last changes fastest.
Arguments:
- activations: bfloat16 [32768, 4096], P(('ctx', 'tp', 'ep')), may hold values from -6 to 6
- output_grad: bfloat16 [32768, 4096], P(('ctx', 'tp', 'ep')), may hold values from -6 to 6
- expert_ids: int32 [32768, 1], P(('ctx', 'tp', 'ep')), may hold values from 0 to 63; in each aligned block of 128 rows (0 to 127, 128 to 255, ...) at most 3 rows name the same one
- gate_values: float32 [32768, 1], P(('ctx', 'tp', 'ep')), may hold values from 0.2 to 1
- keep_mask: int32 [32768, 1], P(('ctx', 'tp', 'ep')), may hold values 0 or 1
- gate_weight: bfloat16 [64, 1536, 4096], P(('tp', 'ep'), 'ctx'), may hold values from -0.09375 to 0.09375
- up_weight: bfloat16 [64, 1536, 4096], P(('tp', 'ep'), 'ctx'), may hold values from -0.09375 to 0.09375
- down_weight: bfloat16 [64, 1536, 4096], P(('tp', 'ep'), 'ctx'), may hold values from -0.15625 to 0.15625
Outputs:
- input_grad: bfloat16 [32768, 4096], P(('ctx', 'tp', 'ep'))
- expert_out: bfloat16 [32768, 4096], P(('ctx', 'tp', 'ep'))
The draws below stay inside these ranges and needn't reach their ends.
Inputs may be any that keep to these rules, and one draw needn't show every extreme that they name: `expert_ids`: no expert is named by more than 3 tokens of one device.
All inputs are finite; a program needn't handle non-finite values. No bound on the sum of `keep_mask` on one device may be relied on, other than what follows from the above.
Results may differ from the reference program's by a relative error of at most 0.015.
Values may be sent and summed in bfloat16 or wider, within the bound.
No kernel may reach another device: no remote copies, remote signals or barrier semaphores. Data moves between devices by JAX's collectives and lax.ppermute only.
A program may use at most 128 MiB of HBM per device.

```python
import math
import jax
import jax.numpy as jnp
import numpy as np
from jax import lax

D = 4096
HIDDEN_SIZE = 1536
TOPK = 1
TOK_DEV = 128
EXPERTS = 64
TOKENS = 32768
CAP = 3
N_CTX = 4


def place_ends(array, own_key, low, high):
    longest = array.shape.index(max(array.shape))
    spots = []
    for shift in (0, 1):
        where = [jax.random.randint(jax.random.fold_in(own_key, axis), (), 0, length) for axis, length in enumerate(array.shape)]
        where[longest] = (where[longest] + shift) % array.shape[longest]
        spots.append(tuple(where))
    return array.at[spots[0]].set(low).at[spots[1]].set(high)


def steps_of(stream_key, extent, cuts, low, high):
    def one(dim, blocks):
        heights = jax.random.uniform(jax.random.fold_in(jax.random.fold_in(stream_key, 6), dim), (blocks,), jnp.float32, low / len(cuts), high / len(cuts))
        return jnp.repeat(jnp.exp(heights), extent[dim] // blocks).reshape((-1,) + (1,) * (len(extent) - dim - 1))

    loudness = one(*cuts[0])
    for cut in cuts[1:]:
        loudness = loudness * one(*cut)
    return loudness


def deal_out(stream_key, own, number, rows, count, top, bound, lean):
    ranking = jax.random.permutation(stream_key, count)
    packed, ordinary = shares(count, rows * top, bound, lean, True), shares(count, rows * top, bound, lean, False)
    places = jnp.arange(count)

    def named(tallies, offset_by):
        used = int((tallies > 0).sum())
        fixed = max(1, used // 4)
        shifted = fixed + (places - fixed + offset_by * (used - fixed)) % max(1, count - fixed)
        return jnp.zeros((count,), jnp.int32).at[ranking[jnp.where(places < fixed, places, shifted)]].set(jnp.asarray(tallies, jnp.int32))

    tallies = jnp.where(number % 4 == 0, named(packed, number // 4), named(ordinary, number - number // 4 - 1))
    mixed = jax.random.permutation(jax.random.fold_in(own, 3), count)
    giver, sink = mixed[0:count // 2 * 2:2], mixed[1:count // 2 * 2:2]
    margin = jnp.minimum(tallies[giver] - 1, bound - tallies[sink]) // 2
    margin = jnp.where((giver == ranking[0]) | (sink == ranking[0]) | (tallies[sink] == 0), 0, jnp.maximum(margin, 0))
    shifted = jax.random.randint(jax.random.fold_in(own, 4), (count // 2,), 0, 1 << 20) % (margin + 1)
    tallies = tallies.at[giver].add(-shifted).at[sink].add(shifted)
    members = jnp.searchsorted(jnp.cumsum(tallies), jnp.arange(rows * top), side="right").astype(jnp.int32)
    listing = members.reshape(top, rows).T
    listing = listing[jax.random.permutation(jax.random.fold_in(own, 1), rows)]
    offset_by = jax.random.randint(jax.random.fold_in(own, 2), (rows, 1), 0, top)
    return jnp.take_along_axis(listing, (jnp.arange(top)[None, :] + offset_by) % top, axis=1)


def shares(count, total, bound, slope, full):
    portions = [(1 << 20) // math.isqrt(standing ** slope) + 1 for standing in range(1, count + 1)]
    largest = bound if full else min(bound, max(-(-total // count), total * portions[0] // sum(portions)))
    least = 1 if total - largest >= count - 1 else 0
    given, rest = [largest] + [least] * (count - 1), total - largest - least * (count - 1)
    while rest > 0:
        movable = [i for i in range(1, count) if given[i] < largest] or [i for i in range(1, count) if given[i] < bound]
        mass, left = sum([portions[i] for i in movable]), rest
        for i in movable:
            addition = min(bound - given[i], max(1, left * portions[i] // mass), rest)
            given[i] = given[i] + addition
            rest = rest - addition
    return np.array(given)


def scatter_about(stream_key, dims, deviation, most, shards=(), held_as=jnp.bfloat16):
    values = deviation * jax.random.normal(stream_key, dims, jnp.float32)
    if shards:
        values = values * steps_of(stream_key, dims, shards, -0.22, 0.18)
    return jnp.clip(values, -most, most).astype(held_as)


def setup_inputs(seed: int = 0) -> dict:
    key_list = jax.random.split(jax.random.key(seed), 9)
    activations = scatter_about(key_list[0], (TOKENS, D), 1.0, 6.0, ((0, 256),))
    output_grad = scatter_about(key_list[1], (TOKENS, D), 1.0, 6.0, ((0, 256),))
    expert_ids_keys = jax.random.split(jax.random.fold_in(key_list[2], 1), TOKENS // TOK_DEV)
    expert_ids_turns = jax.random.permutation(jax.random.fold_in(key_list[2], 3), TOKENS // TOK_DEV)
    expert_ids = jax.vmap(lambda own, number: deal_out(jax.random.fold_in(key_list[2], 2), own, number, TOK_DEV, EXPERTS, TOPK, CAP, 2))(expert_ids_keys, expert_ids_turns).reshape((TOKENS, TOPK))
    gate_values = jnp.clip(0.2 + 0.8 * jax.random.uniform(key_list[3], (TOKENS, TOPK), jnp.float32) ** steps_of(key_list[3], (TOKENS, TOPK), ((0, 256),), -0.2, 0.2), 0.2, 1.0)
    keep_mask = place_ends((jax.random.randint(key_list[4], (TOKENS, TOPK), 0, 8) < 7).astype(jnp.int32), jax.random.fold_in(key_list[4], 1), 0, 1)
    gate_weight = scatter_about(key_list[5], (EXPERTS, HIDDEN_SIZE, D), D ** -0.5, 0.09375, ((0, 64), (1, 4)))
    up_weight = scatter_about(key_list[6], (EXPERTS, HIDDEN_SIZE, D), D ** -0.5, 0.09375, ((0, 64), (1, 4)))
    down_weight = scatter_about(key_list[7], (EXPERTS, HIDDEN_SIZE, D), HIDDEN_SIZE ** -0.5, 0.15625, ((0, 64), (1, 4)))
    return dict(activations=activations, output_grad=output_grad, expert_ids=expert_ids, gate_values=gate_values, keep_mask=keep_mask, gate_weight=gate_weight, up_weight=up_weight, down_weight=down_weight)


def rounded(values):
    return lax.optimization_barrier(values.astype(jnp.bfloat16)).astype(jnp.float32)


def reference(activations, output_grad, expert_ids, gate_values, keep_mask, gate_weight, up_weight, down_weight):
    blocks = TOKENS // TOK_DEV
    slice_width = HIDDEN_SIZE // N_CTX
    assigned = expert_ids.reshape(blocks, TOK_DEV * TOPK)
    kept = keep_mask.reshape(blocks, TOK_DEV * TOPK) == 1
    expert_grid = jnp.arange(EXPERTS, dtype=jnp.int32)
    onehot = ((assigned[:, :, None] == expert_grid[None, None, :]) & kept[:, :, None]).astype(jnp.int32)
    earlier = jnp.cumsum(onehot, axis=1) - onehot
    slot_of = jnp.sum(earlier * onehot, axis=2).astype(jnp.int32)
    row_of = (jnp.arange(blocks, dtype=jnp.int32)[:, None] * CAP + slot_of).reshape(-1).astype(jnp.int32)
    expert_of = jnp.where(kept, assigned, EXPERTS).reshape(-1).astype(jnp.int32)
    token_of = jnp.repeat(jnp.arange(TOKENS, dtype=jnp.int32), TOPK)
    token_table = jnp.full((EXPERTS, blocks * CAP), TOKENS, jnp.int32)
    token_table = token_table.at[expert_of, row_of].set(token_of, mode="drop")
    gate_table = jnp.zeros((EXPERTS, blocks * CAP), jnp.float32)
    gate_table = gate_table.at[expert_of, row_of].set(gate_values.reshape(-1).astype(jnp.float32), mode="drop")

    def split_product(left, weights):
        rows_count = left.shape[0]
        left_split = left.astype(jnp.float32).reshape(rows_count, N_CTX, slice_width)
        right_split = weights.astype(jnp.float32).reshape(N_CTX, slice_width, D)
        return jnp.einsum("rch,chd->rcd", left_split, right_split)

    def per_expert(totals, inputs):
        grad_total, out_total = totals
        rows_token, rows_gate, gate_w, up_w, down_w = inputs
        rows_in = jnp.take(activations, rows_token, axis=0, mode="fill", fill_value=0)
        rows_grad = jnp.take(output_grad, rows_token, axis=0, mode="fill", fill_value=0)
        gate_pre = jnp.dot(rows_in, gate_w.T, preferred_element_type=jnp.float32)
        up_pre = jnp.dot(rows_in, up_w.T, preferred_element_type=jnp.float32)
        sigmoid_gate = jax.nn.sigmoid(gate_pre)
        silu_gate = gate_pre * sigmoid_gate
        hidden = (silu_gate * up_pre).astype(jnp.bfloat16)
        out_slot = jnp.sum(rounded(split_product(hidden, down_w)), axis=1).astype(jnp.bfloat16)
        back_hidden = jnp.dot(rows_grad, down_w.T, preferred_element_type=jnp.float32)
        grad_gate = (back_hidden * up_pre * sigmoid_gate * (1.0 + gate_pre * (1.0 - sigmoid_gate))).astype(jnp.bfloat16)
        grad_up = (back_hidden * silu_gate).astype(jnp.bfloat16)
        grad_parts = split_product(grad_gate, gate_w) + split_product(grad_up, up_w)
        grad_slot = jnp.sum(rounded(grad_parts), axis=1).astype(jnp.bfloat16)
        out_total = out_total.at[rows_token].add(rows_gate[:, None] * out_slot.astype(jnp.float32), mode="drop")
        grad_total = grad_total.at[rows_token].add(rows_gate[:, None] * grad_slot.astype(jnp.float32), mode="drop")
        return (grad_total, out_total), None

    start_totals = (jnp.zeros((TOKENS, D), jnp.float32), jnp.zeros((TOKENS, D), jnp.float32))
    final_totals, unused = lax.scan(per_expert, start_totals, (token_table, gate_table, gate_weight, up_weight, down_weight))
    return (final_totals[0].astype(jnp.bfloat16), final_totals[1].astype(jnp.bfloat16))
```

```python
import jax
import jax.numpy as jnp
from jax import lax
from jax.sharding import PartitionSpec as P

CAP = 3
SUB = 8
F32 = jnp.float32
BF16 = jnp.bfloat16
TRANSPOSED = (((1,), (1,)), ((), ()))
ROWS_FIRST = (((0,), (0,)), ((), ()))


def after(value, *others):
    return lax.optimization_barrier((value, others))[0]


def shift(rows, by):
    count = lax.axis_size("ctx")
    return lax.ppermute(rows, "ctx", [(i, (i + by) % count) for i in range(count)])


def exchange(pair):
    return lax.all_to_all(pair, ("tp", "ep"), split_axis=0, concat_axis=0, tiled=True)


def folded(rows):
    return rows.reshape(rows.shape[0], SUB, rows.shape[1] // SUB)


def flat(rows):
    return rows.reshape(rows.shape[0], -1)


def gather_near(own):
    return shift(own, 1), shift(own, -1)


def gather_far(near):
    before, behind = near
    return shift(before[:, :SUB], 1), shift(behind[:, SUB:], -1)


def gathered(own, near, far):
    before, behind = near
    every_in = jnp.concatenate([own[:, :SUB], before[:, :SUB], behind[:, :SUB], far[0]], axis=0)
    every_grad = jnp.concatenate([own[:, SUB:], before[:, SUB:], behind[:, SUB:], far[1]], axis=0)
    return flat(every_in), flat(every_grad)


def sum_far(parts):
    out_part, grad_part = parts
    quarter = out_part.shape[0] // 4
    return shift(out_part[3 * quarter :], 1), shift(grad_part[3 * quarter :], -1)


def sum_near(parts, got):
    out_part, grad_part = parts
    n = out_part.shape[0] // 4
    out_got = (out_part[2 * n : 3 * n].astype(F32) + got[0].astype(F32)).astype(BF16)
    grad_got = (grad_part[n : 2 * n].astype(F32) + got[1].astype(F32)).astype(BF16)
    to_behind = jnp.concatenate([out_got, grad_part[2 * n : 3 * n]], axis=1)
    to_before = jnp.concatenate([out_part[n : 2 * n], grad_got], axis=1)
    return shift(to_behind, 1), shift(to_before, -1)


def summed(parts, arrived):
    out_part, grad_part = parts
    n = out_part.shape[0] // 4
    own = jnp.concatenate([out_part[:n], grad_part[:n]], axis=1)
    return (own.astype(F32) + arrived[0].astype(F32) + arrived[1].astype(F32)).astype(BF16)


def swiglu_slice(rows, gate_w, up_w, down_w):
    rows_in, rows_grad = rows
    gate_pre = lax.dot_general(rows_in, gate_w, TRANSPOSED, preferred_element_type=F32)
    up_pre = lax.dot_general(rows_in, up_w, TRANSPOSED, preferred_element_type=F32)
    back_hidden = lax.dot_general(rows_grad, down_w, TRANSPOSED, preferred_element_type=F32)
    sigmoid_gate = jax.nn.sigmoid(gate_pre)
    silu_gate = gate_pre * sigmoid_gate
    hidden = (silu_gate * up_pre).astype(BF16)
    grad_gate = (
        back_hidden * up_pre * sigmoid_gate * (1.0 + gate_pre * (1.0 - sigmoid_gate))
    ).astype(BF16)
    grad_up = (back_hidden * silu_gate).astype(BF16)
    out_part = jnp.dot(hidden, down_w, preferred_element_type=F32).astype(BF16)
    grad_part = (
        jnp.dot(grad_gate, gate_w, preferred_element_type=F32)
        + jnp.dot(grad_up, up_w, preferred_element_type=F32)
    ).astype(BF16)
    return folded(out_part), folded(grad_part)


def per_device(
    activations, output_grad, expert_ids, gate_values, keep_mask, gate_weight, up_weight, down_weight
):
    experts_all = lax.axis_size("tp") * lax.axis_size("ep")
    assigned = expert_ids.reshape(-1)
    kept = keep_mask.reshape(-1) == 1
    expert_grid = jnp.arange(experts_all, dtype=jnp.int32)
    named = (assigned[:, None] == expert_grid[None, :]) & kept[:, None]
    onehot = named.astype(jnp.int32)
    earlier = jnp.cumsum(onehot, axis=0) - onehot
    placing = [(named & (earlier == slot)).astype(BF16) for slot in range(CAP)]
    weights = (gate_weight[0], up_weight[0], down_weight[0])

    def placed(slot):
        rows = [
            lax.dot_general(placing[slot], source, ROWS_FIRST, preferred_element_type=F32)
            for source in (activations, output_grad)
        ]
        return jnp.concatenate([folded(r.astype(BF16)) for r in rows], axis=1)

    def token_rows(slot, pair):
        return [
            jnp.dot(placing[slot], flat(half), preferred_element_type=F32)
            for half in (pair[:, SUB:], pair[:, :SUB])
        ]

    own0 = exchange(placed(0))
    own1 = exchange(after(placed(1), own0))
    near0 = gather_near(own0)
    own2 = exchange(after(placed(2), own1, near0))
    far0 = gather_far(near0)
    near1 = gather_near(after(own1, near0))
    parts0 = swiglu_slice(gathered(own0, near0, far0), *weights)
    far1 = gather_far(after(near1, far0))
    got0 = sum_far(after(parts0, near1))
    parts1 = swiglu_slice(gathered(own1, near1, far1), *weights)
    arrived0 = sum_near(parts0, after(got0, far1))
    near2 = gather_near(after(own2, got0))
    back0 = exchange(summed(parts0, arrived0))
    far2 = gather_far(after(near2, arrived0))
    got1 = sum_far(after(parts1, near2))
    arrived1 = sum_near(parts1, after(got1, far2))
    parts2 = swiglu_slice(gathered(own2, near2, far2), *weights)
    got2 = sum_far(after(parts2, got1))
    back1 = exchange(after(summed(parts1, arrived1), back0))
    arrived2 = sum_near(parts2, after(got2, arrived1))
    rows0 = token_rows(0, back0)
    rows1 = token_rows(1, back1)
    back2 = exchange(summed(parts2, arrived2))
    rows2 = token_rows(2, back2)
    weighting = gate_values.astype(F32)
    return tuple(
        (weighting * (a + b + c)).astype(BF16) for a, b, c in zip(rows0, rows1, rows2)
    )


def solution(mesh):
    tokens = P(("ctx", "tp", "ep"), None)
    weights = P(("tp", "ep"), "ctx", None)
    return jax.shard_map(
        per_device,
        mesh=mesh,
        in_specs=(tokens,) * 5 + (weights,) * 3,
        out_specs=(tokens, tokens),
        check_vma=False,
    )
```

```python
from typing import NamedTuple

import jax
import jax.numpy as jnp
from jax import lax
from jax.experimental import pallas as pl
from jax.experimental.pallas import tpu as pltpu
from jax.sharding import PartitionSpec as P

CAP = 3
SUB = 8
F32 = jnp.float32
BF16 = jnp.bfloat16
TRANSPOSED = (((1,), (1,)), ((), ()))
ROWS_FIRST = (((0,), (0,)), ((), ()))


def after(value, *others):
    return lax.optimization_barrier((value, others))[0]


def shift(rows, by):
    count = lax.axis_size("ctx")
    return lax.ppermute(rows, "ctx", [(i, (i + by) % count) for i in range(count)])


def exchange(pair):
    return lax.all_to_all(pair, ("tp", "ep"), split_axis=0, concat_axis=0, tiled=True)


def folded(rows):
    return rows.reshape(rows.shape[0], SUB, rows.shape[1] // SUB)


def flat(rows):
    return rows.reshape(rows.shape[0], -1)


def gather_near(own):
    return shift(own, 1), shift(own, -1)


def gather_far(near):
    before, behind = near
    return shift(before[:, :SUB], 1), shift(behind[:, SUB:], -1)


def sum_first(parts):
    return shift(parts.up, 1), shift(parts.down, -1)


def sum_second(parts, first):
    from_before, from_behind = first
    relay_up = parts.relay_out.astype(F32) + from_before[:, :SUB].astype(F32)
    relay_down = parts.relay_grad.astype(F32) + from_behind[:, SUB:].astype(F32)
    return shift(relay_up.astype(BF16), 1), shift(relay_down.astype(BF16), -1)


def summed(parts, first, second):
    from_before, from_behind = first
    near = jnp.concatenate([from_behind[:, :SUB], from_before[:, SUB:]], axis=1)
    passed = jnp.concatenate(second, axis=1)
    return (parts.own.astype(F32) + near.astype(F32) + passed.astype(F32)).astype(BF16)


class Parts(NamedTuple):
    own: jax.Array
    up: jax.Array
    down: jax.Array
    relay_out: jax.Array
    relay_grad: jax.Array


def expert_kernel(
    own, before, behind, far_in, far_grad, gate_w, up_w, down_w,
    own_parts, up_parts, down_parts, relay_out, relay_grad,
    landed, landed_far, rows_in, rows_grad, product, leaving, leaving_relay, arrive, leave,
):
    experts, width = landed.shape[1], landed.shape[3]
    sources = [(ref, landed.at[i]) for i, ref in enumerate((own, before, behind))]
    sources += [(ref, landed_far.at[i]) for i, ref in enumerate((far_in, far_grad))]
    inward = [
        pltpu.make_async_copy(src, dst, arrive.at[i]) for i, (src, dst) in enumerate(sources)
    ]
    for copy in inward:
        copy.start()
    for block in range(3):
        inward[block].wait()
        here = pl.ds(block * experts, experts)
        rows_in[here, :] = landed[block, :, :SUB, :].reshape(experts, SUB * width)
        rows_grad[here, :] = landed[block, :, SUB:, :].reshape(experts, SUB * width)
    here = pl.ds(3 * experts, experts)
    inward[3].wait()
    rows_in[here, :] = landed_far[0].reshape(experts, SUB * width)
    inward[4].wait()
    rows_grad[here, :] = landed_far[1].reshape(experts, SUB * width)

    gate_pre = lax.dot_general(rows_in[...], gate_w[...], TRANSPOSED, preferred_element_type=F32)
    up_pre = lax.dot_general(rows_in[...], up_w[...], TRANSPOSED, preferred_element_type=F32)
    back_hidden = lax.dot_general(
        rows_grad[...], down_w[...], TRANSPOSED, preferred_element_type=F32
    )
    sigmoid_gate = jax.nn.sigmoid(gate_pre)
    silu_gate = gate_pre * sigmoid_gate
    hidden = (silu_gate * up_pre).astype(BF16)
    grad_gate = (
        back_hidden * up_pre * sigmoid_gate * (1.0 + gate_pre * (1.0 - sigmoid_gate))
    ).astype(BF16)
    grad_up = (back_hidden * silu_gate).astype(BF16)

    def folded_rows(block):
        rows = product[pl.ds(block * experts, experts), :]
        return rows.reshape(experts, SUB, width)

    for j in range(SUB):
        columns = pl.ds(j * width, width)
        product[:, columns] = jnp.dot(
            hidden, down_w[:, columns], preferred_element_type=F32
        ).astype(BF16)
    leaving[1, :, :SUB, :] = folded_rows(3)
    leaving[2, :, :SUB, :] = folded_rows(1)
    leaving_relay[0] = folded_rows(2)
    leaving[0, :, :SUB, :] = folded_rows(0)
    for j in range(SUB):
        columns = pl.ds(j * width, width)
        product[:, columns] = (
            jnp.dot(grad_gate, gate_w[:, columns], preferred_element_type=F32)
            + jnp.dot(grad_up, up_w[:, columns], preferred_element_type=F32)
        ).astype(BF16)
    targets = [
        (leaving.at[1], up_parts), (leaving.at[2], down_parts), (leaving_relay.at[0], relay_out),
        (leaving_relay.at[1], relay_grad), (leaving.at[0], own_parts),
    ]
    outward = [
        pltpu.make_async_copy(src, dst, leave.at[i]) for i, (src, dst) in enumerate(targets)
    ]
    leaving[1, :, SUB:, :] = folded_rows(2)
    outward[0].start()
    leaving[2, :, SUB:, :] = folded_rows(3)
    outward[1].start()
    outward[2].start()
    leaving_relay[1] = folded_rows(1)
    outward[3].start()
    leaving[0, :, SUB:, :] = folded_rows(0)
    outward[4].start()
    for copy in outward:
        copy.wait()


def swiglu_slice(own, near, far, weights):
    experts, both, width = own.shape
    hidden_units, features = weights[0].shape
    pair = jax.ShapeDtypeStruct((experts, both, width), BF16)
    single = jax.ShapeDtypeStruct((experts, SUB, width), BF16)
    vmem = pl.BlockSpec(memory_space=pltpu.VMEM)
    anywhere = pl.BlockSpec(memory_space=pl.ANY)
    rows = 4 * experts
    return Parts(
        *pl.pallas_call(
            expert_kernel,
            out_shape=(pair, pair, pair, single, single),
            in_specs=[anywhere] * 5 + [vmem] * 3,
            out_specs=(anywhere,) * 5,
            scratch_shapes=[
                pltpu.VMEM((3, experts, both, width), BF16),
                pltpu.VMEM((2, experts, SUB, width), BF16),
                pltpu.VMEM((rows, features), BF16),
                pltpu.VMEM((rows, features), BF16),
                pltpu.VMEM((rows, features), BF16),
                pltpu.VMEM((3, experts, both, width), BF16),
                pltpu.VMEM((2, experts, SUB, width), BF16),
                pltpu.SemaphoreType.DMA((5,)),
                pltpu.SemaphoreType.DMA((5,)),
            ],
            cost_estimate=pl.CostEstimate(
                flops=40 * rows * features * hidden_units,
                bytes_accessed=6 * hidden_units * features,
                transcendentals=rows * hidden_units,
            ),
            compiler_params=pltpu.CompilerParams(vmem_limit_bytes=40 * 2**20),
        )(own, *near, *far, *weights)
    )


def per_device(
    activations, output_grad, expert_ids, gate_values, keep_mask, gate_weight, up_weight, down_weight
):
    experts_all = lax.axis_size("tp") * lax.axis_size("ep")
    assigned = expert_ids.reshape(-1)
    kept = keep_mask.reshape(-1) == 1
    expert_grid = jnp.arange(experts_all, dtype=jnp.int32)
    named = (assigned[:, None] == expert_grid[None, :]) & kept[:, None]
    onehot = named.astype(jnp.int32)
    earlier = jnp.cumsum(onehot, axis=0) - onehot
    placing = [(named & (earlier == slot)).astype(BF16) for slot in range(CAP)]
    weights = (gate_weight[0], up_weight[0], down_weight[0])

    def placed(slot):
        rows = [
            lax.dot_general(placing[slot], source, ROWS_FIRST, preferred_element_type=F32)
            for source in (activations, output_grad)
        ]
        return jnp.concatenate([folded(r.astype(BF16)) for r in rows], axis=1)

    def token_rows(slot, pair):
        return [
            jnp.dot(placing[slot], flat(half), preferred_element_type=F32)
            for half in (pair[:, SUB:], pair[:, :SUB])
        ]

    own0 = exchange(placed(0))
    send1, send2 = placed(1), placed(2)
    own1 = exchange(after(send1, own0, send2))
    near0 = gather_near(own0)
    own2 = exchange(after(send2, own1))
    far0 = gather_far(near0)
    near1 = gather_near(after(own1, near0))
    far1 = gather_far(after(near1, far0))
    near2 = gather_near(after(own2, near1))
    parts0 = swiglu_slice(own0, near0, far0, weights)
    first0 = sum_first(after(parts0, far1))
    parts1 = swiglu_slice(own1, near1, far1, weights)
    far2 = gather_far(after(near2, far1))
    second0 = sum_second(parts0, after(first0, near2))
    first1 = sum_first(after(parts1, far2))
    back0 = exchange(summed(parts0, first0, second0))
    parts2 = swiglu_slice(own2, near2, far2, weights)
    second1 = sum_second(parts1, after(first1, second0))
    first2 = sum_first(after(parts2, first1))
    back1 = exchange(after(summed(parts1, first1, second1), back0))
    second2 = sum_second(parts2, after(first2, second1))
    rows0 = token_rows(0, back0)
    rows1 = token_rows(1, back1)
    back2 = exchange(after(summed(parts2, first2, second2), back1))
    rows2 = token_rows(2, back2)
    weighting = gate_values.astype(F32)
    return tuple(
        (weighting * (a + b + c)).astype(BF16) for a, b, c in zip(rows0, rows1, rows2)
    )


def solution(mesh):
    tokens = P(("ctx", "tp", "ep"), None)
    weights = P(("tp", "ep"), "ctx", None)
    return jax.shard_map(
        per_device,
        mesh=mesh,
        in_specs=(tokens,) * 5 + (weights,) * 3,
        out_specs=(tokens, tokens),
        check_vma=False,
    )
```
